32 devices in a mesh: mem: 4 (over z), patch: 8 (over y, x, core).
Axes of the slice: x: 2, y: 2, z: 4, core: 2. Of those that a mesh axis runs over, the one named last changes fastest.
Arguments:
- ensemble: bfloat16 [1024, 12, 4096], P(('mem', 'patch')), may hold values from -6 to 6
- obs_col: int32 [4096], replicated, may hold values from 0 to 4095, as said below
- obs_var: int32 [4096], replicated, may hold values from 0 to 11
- obs_value: float32 [4096], replicated, may hold values from -8 to 8
- obs_err: float32 [4096], replicated, may hold values from 0.5 to 2
- obs_count: int32 [32], replicated, may hold values from 32 to 128, as said below
- coarse_list: int32 [128, 128], P(('mem', 'patch')), may hold values from 0 to 383, as said below
- coarse_count: int32 [128], P(('mem', 'patch')), may hold values from 32 to 128, as said below
Outputs:
- analysis: bfloat16 [1024, 12, 4096], P(('mem', 'patch'))
The draws below stay inside these ranges and needn't reach their ends.
Inputs may be any that keep to these rules, and one draw needn't show every extreme that they name: `obs_col`: slot j lies in column block j // 128, so its column is between (j // 128) * 128 and that plus 128 - 1. `obs_count`: patches whose index is 0 mod 4 hold 128 observations, those 2 mod 4 hold 32, the others between 64 and 128. `coarse_list`: entries of one row are distinct window rows of the coarse point's patch, all of present observations. `coarse_count`: the first coarse point of every patch uses all 128 slots.
All inputs are finite; a program needn't handle non-finite values. Where the reference program divides by a largest or mean magnitude, that divisor is 1e-20 or more.
Results may differ from the reference program's by a relative error of at most 0.0017.
Values may be sent and summed in bfloat16 or wider, within the bound.
No kernel may reach another device: no remote copies, remote signals or barrier semaphores. Data moves between devices by JAX's collectives and lax.ppermute only.
A program may use at most 192 MiB of HBM per device.

```python
import math
import jax
import jax.numpy as jnp
from jax import lax

K = 1024
F = 12
COL_DEV = 128
OBS_DEV = 128
P_SIZE = 128
NS_STEPS = 4
NCG = 4
NPATCHES = 32
NCOL = 4096
NOBS = 4096
NCOARSE = 128
N_MEM = 4
N_PATCH = 8


def patch_counts(key):
    drawn = jax.random.randint(key, (NPATCHES,), OBS_DEV // 2, OBS_DEV + 1, dtype=jnp.int32)
    phase = jnp.arange(NPATCHES, dtype=jnp.int32) % 4
    full = jnp.full((NPATCHES,), OBS_DEV, dtype=jnp.int32)
    sparse = jnp.full((NPATCHES,), OBS_DEV // 4, dtype=jnp.int32)
    return jnp.where(phase == 0, full, jnp.where(phase == 2, sparse, drawn)).astype(jnp.int32)


def draw_obs_count(key, part):
    counts = patch_counts(key)
    return counts


def draw_obs_col(key, part):
    key = jax.random.fold_in(key, 11)
    block_index = jnp.arange(NOBS, dtype=jnp.int32) // OBS_DEV
    return (block_index * COL_DEV + jax.random.randint(key, (NOBS,), 0, COL_DEV, dtype=jnp.int32)).astype(jnp.int32)


def draw_coarse_list(key, part):
    counts = patch_counts(key)
    key = jax.random.fold_in(key, 12)
    row_keys = jax.random.split(key, NCOARSE)
    window_slot = jnp.arange(3 * OBS_DEV, dtype=jnp.int32)
    patch_of = jnp.arange(NCOARSE, dtype=jnp.int32) // NCG

    def pick_row(row_key, patch_index):
        owner = (patch_index - 1 + window_slot // OBS_DEV) % NPATCHES
        present = window_slot % OBS_DEV < counts[owner]
        order = jax.random.permutation(row_key, 3 * OBS_DEV).astype(jnp.int32)
        score = jnp.where(present, order, order + 3 * OBS_DEV)
        return jnp.argsort(score)[:P_SIZE]
    return jax.vmap(pick_row)(row_keys, patch_of).astype(jnp.int32)


def draw_coarse_count(key, part):
    key = jax.random.fold_in(key, 13)
    drawn = jax.random.randint(key, (NCOARSE,), P_SIZE // 4, P_SIZE + 1, dtype=jnp.int32)
    first_point = jnp.arange(NCOARSE, dtype=jnp.int32) % NCG == 0
    return jnp.where(first_point, P_SIZE, drawn).astype(jnp.int32)


def with_ends(result, rng, least, top_value):
    extent = result.shape
    place = [jax.random.randint(jax.random.fold_in(rng, axis), (), 0, extent[axis]) for axis in range(len(extent))]
    result = result.at[tuple(place)].set(least)
    longest = extent.index(max(extent))
    place[longest] = (place[longest] + 1) % extent[longest]
    return result.at[tuple(place)].set(top_value)


def block_scale(rng, shape, shards, low, largest):
    loudness, own = 1.0, jax.random.fold_in(rng, 6)
    for position, parts in shards:
        heights = jnp.exp(jax.random.uniform(jax.random.fold_in(own, position), (parts,), jnp.float32, low / len(shards), largest / len(shards)))
        loudness = loudness * jnp.repeat(heights, shape[position] // parts).reshape([-1 if axis == position else 1 for axis in range(len(shape))])
    return loudness


def noise(stream_key, dims, deviation, limit, pieces=(), kind=jnp.bfloat16):
    level = block_scale(stream_key, dims, pieces, -0.22, 0.18) if pieces else 1.0
    values = jax.random.normal(stream_key, dims, jnp.float32) * deviation * level
    return jnp.minimum(jnp.maximum(values, -limit), limit).astype(kind)


def setup_inputs(seed: int = 0) -> dict:
    keys = jax.random.split(jax.random.key(seed), 9)
    ensemble = noise(keys[0], (K, F, NCOL), 1.0, 6.0, ((0, 32),))
    obs_col = draw_obs_col(jax.random.fold_in(keys[8], 71), 0)
    obs_var = with_ends(jax.random.randint(keys[2], (NOBS,), 0, F), jax.random.fold_in(keys[2], 1), 0, F - 1).astype(jnp.int32)
    obs_value = noise(keys[3], (NOBS,), 1.5, 8.0, (), jnp.float32)
    obs_err = jnp.clip(jnp.exp(jax.random.uniform(keys[4], (NOBS,), jnp.float32, math.log(0.5), math.log(2.0))), 0.5, 2.0)
    obs_count = draw_obs_count(jax.random.fold_in(keys[8], 71), 0)
    coarse_list = draw_coarse_list(jax.random.fold_in(keys[8], 71), 0)
    coarse_count = draw_coarse_count(jax.random.fold_in(keys[8], 71), 0)
    return dict(ensemble=ensemble, obs_col=obs_col, obs_var=obs_var, obs_value=obs_value, obs_err=obs_err, obs_count=obs_count, coarse_list=coarse_list, coarse_count=coarse_count)


def analyse(background, window_rows, values, errors, columns, present, lists, counts, first_column, total_columns):
    f32 = jnp.float32
    highest = lax.Precision.HIGHEST
    members, fields, col_count = background.shape
    blocks, slots = lists.shape
    group = col_count // blocks
    dof_ratio = members - 1.0
    row_mean = lax.optimization_barrier(jnp.mean(window_rows.astype(f32), axis=0))
    obs_pert = (window_rows.astype(f32) - row_mean[None, :]).astype(jnp.bfloat16)
    innov = values - row_mean
    field_mean = lax.optimization_barrier(jnp.mean(background.astype(f32), axis=0))
    field_pert = (background.astype(f32) - field_mean[None, :, :]).astype(jnp.bfloat16)
    live_slot = (jnp.arange(slots, dtype=jnp.int32)[None, :] < counts[:, None]) & present[lists]
    centre = (first_column + group * jnp.arange(blocks, dtype=jnp.int32)).astype(f32) + 0.5 * (group - 1)
    offset = columns[lists].astype(f32) - centre[:, None]
    offset = offset - total_columns * jnp.floor(offset / total_columns + 0.5)
    weight = jnp.where(live_slot, jnp.exp(-(offset / col_count) ** 2) / errors[lists], 0.0).astype(f32)
    flat_list = lists.reshape(-1)
    picked = obs_pert[:, flat_list].astype(f32)
    full_gram = lax.dot_general(picked, picked, (((0,), (0,)), ((), ())), precision=highest)
    block_ids = jnp.arange(blocks, dtype=jnp.int32)
    gram = full_gram.reshape(blocks, slots, blocks, slots)[block_ids, :, block_ids, :]
    identity = jnp.eye(slots, dtype=f32)
    bmat = identity + weight[:, :, None] * gram * weight[:, None, :] / dof_ratio
    scale = lax.optimization_barrier(jnp.max(lax.optimization_barrier(jnp.sum(jnp.abs(bmat), axis=2)), axis=1))
    ymat = bmat / scale[:, None, None]
    zmat = jnp.broadcast_to(identity, bmat.shape)
    for newton_step in range(NS_STEPS):
        tmat = 0.5 * (3.0 * identity - jnp.matmul(zmat, ymat, precision=highest))
        ymat = jnp.matmul(ymat, tmat, precision=highest)
        zmat = jnp.matmul(tmat, zmat, precision=highest)
    root = jnp.sqrt(scale)[:, None, None] * ymat
    stacked = jnp.concatenate([bmat, bmat + root], axis=0)
    lowers = jnp.linalg.cholesky(stacked)
    inv_lowers = jax.scipy.linalg.solve_triangular(lowers, jnp.broadcast_to(identity, stacked.shape), lower=True)
    inv_b = inv_lowers[:blocks]
    inv_hl = inv_lowers[blocks:]
    inverse_h = jnp.matmul(jnp.swapaxes(inv_hl, 1, 2), inv_hl, precision=highest)
    rhs = weight * innov[lists]
    half = jnp.einsum('gij,gj->gi', inv_b, rhs, precision=highest)
    mean_weight = jnp.einsum('gji,gj->gi', inv_b, half, precision=highest) / dof_ratio
    mix = -(weight[:, :, None] * inverse_h * weight[:, None, :]) / dof_ratio
    shift_flat = (weight * mean_weight).reshape(-1)
    wide = fields * col_count
    pert_flat = field_pert.reshape(members, wide).astype(f32)
    proj = lax.dot_general(picked, pert_flat, (((0,), (0,)), ((), ())), precision=highest)
    own = (jnp.arange(blocks * slots, dtype=jnp.int32) // slots)[:, None] == (jnp.arange(col_count, dtype=jnp.int32) // group)[None, :]
    masked = jnp.where(own[:, None, :], proj.reshape(blocks * slots, fields, col_count), 0.0).reshape(blocks * slots, wide)
    mean_term = jnp.dot(shift_flat, masked, precision=highest)
    eye_blocks = jnp.eye(blocks, dtype=f32)
    mix_full = (eye_blocks[:, None, :, None] * mix[:, :, None, :]).reshape(blocks * slots, blocks * slots)
    spread_term = lax.dot_general(mix_full, masked, (((0,), (0,)), ((), ())), precision=highest).astype(jnp.bfloat16)
    update = jnp.dot(picked, spread_term.astype(f32), precision=highest)
    total = background.reshape(members, wide).astype(f32) + mean_term[None, :] + update
    return total.astype(jnp.bfloat16).reshape(members, fields, col_count)

def reference(ensemble, obs_col, obs_var, obs_value, obs_err, obs_count, coarse_list, coarse_count):
    devices = N_MEM * N_PATCH
    total_columns = COL_DEV * devices
    window_slot = jnp.arange(3 * OBS_DEV, dtype=jnp.int32)

    def one_patch(device_index):
        background = lax.dynamic_slice_in_dim(ensemble, (device_index * COL_DEV).astype(jnp.int32), COL_DEV, 2)
        owner = ((device_index - 1 + window_slot // OBS_DEV) % devices).astype(jnp.int32)
        window_index = (owner * OBS_DEV + window_slot % OBS_DEV).astype(jnp.int32)
        present = window_slot % OBS_DEV < obs_count[owner]
        window_rows = ensemble[:, obs_var[window_index], obs_col[window_index]]
        lists = lax.dynamic_slice_in_dim(coarse_list, (device_index * NCG).astype(jnp.int32), NCG, 0)
        counts = lax.dynamic_slice_in_dim(coarse_count, (device_index * NCG).astype(jnp.int32), NCG, 0)
        return analyse(background, window_rows, obs_value[window_index], obs_err[window_index], obs_col[window_index], present, lists, counts, (device_index * COL_DEV).astype(jnp.int32), float(total_columns))
    stacked = lax.map(one_patch, jnp.arange(devices, dtype=jnp.int32))
    return stacked.transpose(1, 2, 0, 3).reshape(K, F, total_columns)
```

```python
import functools

import jax
import jax.numpy as jnp
from jax import lax
from jax.experimental import pallas as pl
from jax.experimental.pallas import tpu as pltpu
from jax.sharding import PartitionSpec as P

OBS_DEV = 128
TAIL = 16
NS_STEPS = 4
AXES = ("mem", "patch")
MIB = 1 << 20
F32 = jnp.float32
BF16 = jnp.bfloat16


def dot16(left, right):
    return lax.dot_general(left, right, (((1,), (0,)), ((), ())), preferred_element_type=F32)


def thirds(value):
    high = value.astype(BF16)
    rest = value - high.astype(F32)
    middle = rest.astype(BF16)
    return high, middle, (rest - middle.astype(F32)).astype(BF16)


def stacked(right):
    high, middle, low = thirds(right)
    return jnp.concatenate([high, middle], axis=0), jnp.concatenate([low, high], axis=0)


def dot32(left, right):
    first, second = right if isinstance(right, tuple) else stacked(right)
    high, middle, low = thirds(left)
    large = dot16(jnp.concatenate([high, high], axis=1), first)
    small = dot16(jnp.concatenate([middle, middle], axis=1), first)
    return large + (small + dot16(jnp.concatenate([high, low], axis=1), second))


def invert_all(a_ref, width):
    matrices, size, _ = a_ref.shape
    count = size // width
    packs = [range(first, first + count) for first in range(0, matrices, count)]
    row = lax.broadcasted_iota(jnp.int32, (size, size), 0)
    lane = lax.broadcasted_iota(jnp.int32, (size, size), 1)
    sub_small = lax.broadcasted_iota(jnp.int32, (width, size), 0)
    lane_small = lax.broadcasted_iota(jnp.int32, (width, size), 1)
    segment = lane_small // width
    within = lane_small - segment * width
    diagonal = (row // width) == (lane // width)
    minus_unit = -((row == lane).astype(F32))

    def block(j, carry):
        start = pl.multiple_of(j * width, width)
        turns = [lax.rem(m * width + size - start, size) for m in range(count)]
        slabs, tops = [], []
        for pack in packs:
            slab = [a_ref[m, pl.ds(start, width), :] for m in pack]
            packed = jnp.zeros((width, size), F32)
            for m in range(count):
                packed = jnp.where(segment == m, pltpu.roll(slab[m], turns[m], 1), packed)
            slabs.append(slab)
            tops.append(packed)
        for k in range(0, width, 2):
            for p, packed in enumerate(tops):
                one = jnp.take_along_axis(packed, segment * width + k, axis=1)
                two = jnp.take_along_axis(packed, segment * width + (k + 1), axis=1)
                a, b = one[k : k + 1, :], two[k : k + 1, :]
                c, d = one[k + 1 : k + 2, :], two[k + 1 : k + 2, :]
                scale = 1.0 / (a * d - b * c)
                at = within[0:1, :]
                upper = jnp.where((at == k) | (at == k + 1), 0.0, packed[k : k + 1, :])
                upper = jnp.where(at == k, 1.0, upper)
                lower = jnp.where((at == k) | (at == k + 1), 0.0, packed[k + 1 : k + 2, :])
                lower = jnp.where(at == k + 1, 1.0, lower)
                first = (d * upper - b * lower) * scale
                second = (a * lower - c * upper) * scale
                pair = (sub_small == k) | (sub_small == k + 1)
                one = jnp.where(pair, jnp.where(sub_small == k, -1.0, 0.0), one)
                two = jnp.where(pair, jnp.where(sub_small == k, 0.0, -1.0), two)
                rest = jnp.where(pair | (within == k) | (within == k + 1), 0.0, packed)
                tops[p] = rest - (one * first + two * second)
        here = lane_small - start
        inside = (here >= 0) & (here < width)
        unit = (here == sub_small).astype(F32)
        in_row = (row >= start) & (row < start + width)
        in_lane = (lane >= start) & (lane < start + width)
        for pack, slab, packed in zip(packs, slabs, tops):
            left = jnp.where(diagonal, jnp.concatenate([packed] * count, axis=0), 0.0)
            right = jnp.concatenate([jnp.where(inside, unit, each) for each in slab], axis=0)
            strip = stacked(dot32(left, right))
            for i, m in enumerate(pack):
                full = a_ref[m]
                head = jnp.where(in_lane, jnp.where(in_row, minus_unit, full), 0.0)
                head = pltpu.roll(head, turns[i], 1)
                a_ref[m] = jnp.where(in_row | in_lane, 0.0, full) - dot32(head, strip)
        return carry

    lax.fori_loop(0, size // width, block, 0)


def parts_of(value):
    parts = []
    for _ in range(3):
        part = value.astype(BF16).astype(F32)
        parts.append(part)
        value = value - part
    return parts


def sum_units(fields, members):
    return -(-3 * fields // members)


def split_kernel(per_step, width, ens_ref, var_ref, col_ref, send_ref, later_ref, head_ref, sems):
    half, _, units, _, _ = send_ref.shape
    devices = 2 * half
    later = later_ref.shape[2]
    fields, members, _ = ens_ref.shape
    early = fields - later
    extra = units - 3 - early
    step = pl.program_id(0)
    copies = []
    for q in range(per_step):
        patch = step * per_step + q
        spot = (lax.rem(patch, half), patch // half)
        lanes = slice(q * width, (q + 1) * width)
        first = send_ref.at[spot[0], spot[1], pl.ds(3 + extra, early)]
        second = later_ref.at[spot[0], spot[1]]
        copies += [
            pltpu.make_async_copy(ens_ref.at[:early, :, lanes], first, sems.at[0, q]),
            pltpu.make_async_copy(ens_ref.at[early:, :, lanes], second, sems.at[1, q]),
        ]
    for copy in copies:
        copy.start()
    place = lax.broadcasted_iota(jnp.int32, (width, OBS_DEV), 0)
    for q in range(per_step):
        patch = step * per_step + q
        spot = (lax.rem(patch, half), patch // half)
        piece = ens_ref[:, :, q * width : (q + 1) * width]
        wide = piece.astype(F32)
        parts = parts_of(jnp.sum(wide[early:], axis=1))
        parts.append(jnp.zeros((extra * members - 3 * later, width), F32))
        parts = jnp.concatenate(parts, axis=0).astype(BF16)
        for u in range(extra):
            head_ref[spot[0], spot[1], 3 + u] = parts[u * members : (u + 1) * members]
        column = col_ref[pl.ds(patch, 1), :] - patch * width
        variable = var_ref[pl.ds(patch, 1), :]
        pick = (place == column).astype(F32).astype(BF16)
        values = dot16(wide.reshape(fields * members, width).astype(BF16), pick)
        taken = jnp.zeros((members, OBS_DEV), F32)
        for f in range(fields):
            taken = jnp.where(variable == f, values[f * members : (f + 1) * members], taken)
        taken = taken.astype(BF16)
        for b in range(3):
            window = lax.rem(patch + (devices + 1 - b), devices)
            head_ref[lax.rem(window, half), window // half, b] = taken
    for copy in copies:
        copy.wait()

    @pl.when(step == devices // per_step - 1)
    def _():
        target = send_ref.at[:, :, pl.ds(0, 3 + extra)]
        copy = pltpu.make_async_copy(head_ref, target, sems.at[0, 0])
        copy.start()
        copy.wait()


def split(ensemble, obs_var, obs_col, devices, early):
    fields, members, columns = ensemble.shape
    width = columns // devices
    per_step = 8
    later = fields - early
    units = (3 + sum_units(later, members) + early, later)
    shapes = [(devices // 2, 2, count, members, width) for count in units]
    return pl.pallas_call(
        functools.partial(split_kernel, per_step, width),
        grid=(devices // per_step,),
        in_specs=[
            pl.BlockSpec((fields, members, per_step * width), lambda i: (0, 0, i)),
            pl.BlockSpec((devices, OBS_DEV), lambda i: (0, 0)),
            pl.BlockSpec((devices, OBS_DEV), lambda i: (0, 0)),
        ],
        out_specs=[pl.BlockSpec(memory_space=pltpu.HBM)] * 2,
        out_shape=[jax.ShapeDtypeStruct(shape, BF16) for shape in shapes],
        scratch_shapes=[
            pltpu.VMEM((devices // 2, 2, units[0] - early, members, width), BF16),
            pltpu.SemaphoreType.DMA((2, per_step)),
        ],
        compiler_params=pltpu.CompilerParams(vmem_limit_bytes=56 * MIB),
        name="split",
    )(ensemble, obs_var, obs_col)


def call(kernel, name, outs, scalars, arrays, scratch=(), flops=10**9):
    whole = lambda array: pl.BlockSpec(array.shape, lambda i: (0,) * len(array.shape))
    outs = [jax.ShapeDtypeStruct(shape, dtype) for shape, dtype in outs]
    return pl.pallas_call(
        kernel,
        grid=(1,),
        in_specs=[pl.BlockSpec(memory_space=pltpu.SMEM)] * len(scalars)
        + [whole(array) for array in arrays],
        out_specs=[whole(out) for out in outs],
        out_shape=outs,
        scratch_shapes=list(scratch),
        compiler_params=pltpu.CompilerParams(vmem_limit_bytes=24 * MIB),
        cost_estimate=pl.CostEstimate(flops=flops, bytes_accessed=MIB, transcendentals=0),
        name=name,
    )(*scalars, *arrays)


def sums_kernel(later, side_ref, x_ref, lists_ref, out_ref, copy_ref):
    _, _, units, local, width = x_ref.shape
    extra = sum_units(later, local)
    copy_ref[...] = x_ref[...]
    for r in range(2):
        whole = jnp.sum(x_ref[:, side_ref[0] ^ r].astype(F32), axis=0)
        parts = whole[3 : 3 + extra].reshape(extra * local, width)
        out_ref[r, 0:3] = jnp.sum(whole[0:3], axis=1)
        early = units - extra
        out_ref[r, 3:early] = jnp.sum(whole[3 + extra :], axis=1)
        total = (parts[0:later] + parts[later : 2 * later]) + parts[2 * later : 3 * later]
        out_ref[r, early : early + later] = total
        out_ref[r, early + later :] = lists_ref[...].astype(F32)


def sums(side, x, lists, later):
    _, _, units, local, width = x.shape
    rows = units - sum_units(later, local) + later + lists.shape[0]
    outs = [((2, rows, width), F32), (x.shape, BF16)]
    return call(functools.partial(sums_kernel, later), "sums", outs, [side], [x, lists])


def picks_kernel(r, side_ref, rows_ref, sum_ref, got_ref, lists_ref, *out_refs):
    picked_ref, turned_ref, gram_ref, *mean_refs = out_refs
    half, _, _, local, _ = rows_ref.shape
    members = half * local
    blocks, slots = lists_ref.shape
    after = sum_ref.shape[1] - blocks
    window_row = lax.broadcasted_iota(jnp.int32, (3 * OBS_DEV, slots), 0)
    mean = (sum_ref[r, 0:3] + got_ref[1 - r, 0:3]) / (2 * members)
    lists = got_ref[0, after:].astype(jnp.int32) if r else lists_ref[...]
    for mean_ref in mean_refs:
        mean_ref[...] = mean
    perts, grams = [], []
    for b in range(3):
        rows = rows_ref[:, side_ref[0] ^ r, b].astype(F32).reshape(members, OBS_DEV)
        perts.append((rows - mean[b : b + 1, :]).astype(BF16))
    pert = jnp.concatenate(perts, axis=1)
    for g in range(blocks):
        choose = (window_row == lists[g : g + 1, :]).astype(F32).astype(BF16)
        picked32 = dot16(pert, choose)
        picked = picked32.astype(BF16)
        turned = picked32.T.astype(BF16)
        piece = slice(g * slots, (g + 1) * slots)
        picked_ref[:, piece] = picked
        turned_ref[piece, :] = turned
        grams.append(dot16(turned, picked))
    if r == 0:
        gram_ref[...] = jnp.concatenate(grams, axis=0)
        return
    lane = lax.broadcasted_iota(jnp.int32, (slots, slots), 1)
    row = lax.broadcasted_iota(jnp.int32, (slots, slots), 0)
    rest = []
    for g in range(0, blocks, 2):
        piece = slice(g // 2 * slots, (g // 2 + 1) * slots)
        gram_ref[piece, :] = jnp.where(row <= lane, grams[g], grams[g + 1])
        diagonal = jnp.where(row == lane, grams[g + 1], 0.0)
        rest.append(jnp.sum(diagonal, axis=0, keepdims=True))
    rest.append(jnp.zeros((8 - blocks // 2, slots), F32))
    gram_ref[blocks // 2 * slots :, :] = jnp.concatenate(rest, axis=0)


def picks(r, side, rows, total, got, lists):
    half, _, _, local, _ = rows.shape
    blocks, slots = lists.shape
    members, wide = half * local, blocks * slots
    outs = [((members, wide), BF16), ((wide, members), BF16)]
    outs += [((wide // 2 + 8, slots), F32)] if r else [((wide, slots), F32), ((3, OBS_DEV), F32)]
    kernel = functools.partial(picks_kernel, r)
    return call(kernel, "picks", outs, [side], [rows, total, got, lists], flops=2 * 10**9)


def weights_kernel(
    members,
    total_columns,
    me_ref,
    obs_count_ref,
    live_ref,
    lists_ref,
    value_ref,
    err_ref,
    col_ref,
    mean_ref,
    gram_ref,
    got_ref,
    mix_ref,
    shift_ref,
    a_ref,
):
    devices = value_ref.shape[0]
    blocks, slots = lists_ref.shape
    col_count = shift_ref.shape[1]
    group = col_count // blocks
    dof = members - 1.0
    window = 3 * OBS_DEV
    me = me_ref[0]
    lane_row = lax.broadcasted_iota(jnp.int32, (1, OBS_DEV), 1)
    means, values, errors, columns, presents = [], [], [], [], []
    for b in range(3):
        owner = lax.rem(me + (b - 1 + devices), devices)
        means.append(mean_ref[b : b + 1, :])
        values.append(value_ref[pl.ds(owner, 1), :])
        errors.append(err_ref[pl.ds(owner, 1), :])
        columns.append(col_ref[pl.ds(owner, 1), :].astype(F32))
        presents.append((lane_row < obs_count_ref[owner]).astype(F32))
    table = jnp.concatenate(
        [jnp.concatenate(x, axis=1) for x in (values, errors, columns, presents, means)]
        + [jnp.zeros((3, window), F32)],
        axis=0,
    )
    lane = lax.broadcasted_iota(jnp.int32, (slots, slots), 1)
    row = lax.broadcasted_iota(jnp.int32, (slots, slots), 0)
    unit = (row == lane).astype(F32)
    window_row = lax.broadcasted_iota(jnp.int32, (window, slots), 0)
    bmats, scales, wides, rhs = [], [], [], []
    for g in range(blocks):
        choose = (window_row == lists_ref[g : g + 1, :]).astype(F32)
        listed = dot32(table, choose)
        value, error, column, present, mean = [listed[i : i + 1, :] for i in range(5)]
        first = (me * col_count + group * g).astype(F32) + 0.5 * (group - 1)
        offset = column - first
        offset = offset - total_columns * jnp.floor(offset / total_columns + 0.5)
        live = (lane_row < live_ref[g]) & (present > 0.5)
        weight = jnp.where(live, jnp.exp(-((offset / col_count) ** 2)) / error, 0.0)
        rhs.append(weight * (value - mean))
        wide = jnp.broadcast_to(weight, (slots, slots))
        wides.append((wide, wide.T))
        piece = slice(g * slots, (g + 1) * slots)
        square = got_ref[g // 2 * slots : (g // 2 + 1) * slots, :]
        if g % 2 == 0:
            other = jnp.where(row <= lane, square, square.T)
        else:
            place = blocks // 2 * slots + g // 2
            other = jnp.where(row > lane, square, square.T)
            other = jnp.where(row == lane, got_ref[place : place + 1, :], other)
        gram = gram_ref[piece, :] + other
        bmat = unit + wides[g][1] * gram * wide / dof
        scales.append(jnp.max(jnp.sum(jnp.abs(bmat), axis=0, keepdims=True), axis=1, keepdims=True))
        bmats.append(bmat)
    every = range(blocks)
    ymats = [bmats[g] / scales[g] for g in every]
    zmats = [None] * blocks
    for step in range(NS_STEPS):
        if step == 0:
            tmats = [0.5 * (3.0 * unit - ymats[g]) for g in every]
        else:
            products = [dot32(zmats[g], ymats[g]) for g in every]
            tmats = [0.5 * (3.0 * unit - products[g]) for g in every]
        ymats = [dot32(ymats[g], tmats[g]) for g in every]
        if step == 0:
            zmats = tmats
        elif step < NS_STEPS - 1:
            zmats = [dot32(tmats[g], zmats[g]) for g in every]
    for g in every:
        a_ref[g] = bmats[g]
        a_ref[blocks + g] = bmats[g] + jnp.sqrt(scales[g]) * ymats[g]
    invert_all(a_ref, slots // blocks)
    shift = jnp.zeros((slots, col_count), F32)
    group_of = lax.broadcasted_iota(jnp.int32, (slots, col_count), 1) // group
    for g in every:
        wide, tall = wides[g]
        mean_weight = jnp.sum(a_ref[g] * rhs[g], axis=1, keepdims=True) / dof
        shift = jnp.where(group_of == g, tall[:, 0:1] * mean_weight, shift)
        mix = -(tall * a_ref[blocks + g] * wide) / dof
        mix_ref[g * slots : (g + 1) * slots, :] = mix.T
    shift_ref[...] = shift


def weights(me, obs_count, live, lists, value, err, col, mean, gram, got, members, total):
    blocks, slots = lists.shape
    width = total // value.shape[0]
    outs = [((blocks * slots, slots), F32), ((slots, width), F32)]
    return call(
        functools.partial(weights_kernel, members, float(total)),
        "weights",
        outs,
        [me, obs_count, live],
        [lists, value, err, col, mean, gram, got],
        [pltpu.VMEM((2 * blocks, slots, slots), F32)],
        flops=8 * 10**10,
    )


def lane_groups(slots, some, width, blocks):
    place = lax.broadcasted_iota(jnp.int32, (slots, some * width), 1)
    return lax.rem(place // (width // blocks), blocks)


def own_blocks(tall, group_of, blocks):
    slots = group_of.shape[0]
    own = tall[0:slots]
    for g in range(1, blocks):
        own = jnp.where(group_of == g, tall[g * slots : (g + 1) * slots], own)
    return own


def side_by_side(x_ref, j, first, some):
    half, _, _, local, width = x_ref.shape
    rows = half * local
    pieces = [x_ref[:, j, first + i].astype(F32).reshape(rows, width) for i in range(some)]
    return jnp.concatenate(pieces, axis=1)


def project_kernel(blocks, first, row, side_ref, x_ref, *rest):
    sum_ref, got_ref, turned_ref, turned_theirs_ref, mine_ref, theirs_ref = rest
    half, _, units, local, width = x_ref.shape
    members = half * local
    some = units - first
    group_of = lane_groups(mine_ref.shape[0], some, width, blocks)
    sides = ((1, turned_theirs_ref, theirs_ref), (0, turned_ref, mine_ref))
    for r, turn_ref, out_ref in sides:
        mean = (sum_ref[r] + got_ref[1 - r]) / (2 * members)
        mean = jnp.concatenate([mean[row + i : row + i + 1, :] for i in range(some)], axis=1)
        pert = (side_by_side(x_ref, side_ref[0] ^ r, first, some) - mean).astype(BF16)
        own = own_blocks(dot16(turn_ref[...], pert), group_of, blocks)
        out_ref[...] = own.astype(out_ref.dtype)


def project(side, x, sum_x, got_x, turned, turned_theirs, blocks, first, row):
    _, _, units, _, width = x.shape
    shape = (turned.shape[0] // blocks, (units - first) * width)
    kernel = functools.partial(project_kernel, blocks, first, row)
    arrays = [x, sum_x, got_x, turned, turned_theirs]
    return call(kernel, "project", [(shape, F32), (shape, BF16)], [side], arrays, flops=2 * 10**9)


def spread_kernel(blocks, mine_ref, got_ref, mix_ref, shift_ref, out_ref):
    slots, width = shift_ref.shape
    lanes = mine_ref.shape[1]
    some = lanes // width
    own = mine_ref[...] + got_ref[...].astype(F32)
    group_of = lane_groups(slots, some, width, blocks)
    shift = jnp.concatenate([shift_ref[...]] * some, axis=1)
    rest = jnp.sum(shift * own, axis=0, keepdims=True)
    out_ref[0:slots, :] = own_blocks(dot32(mix_ref[...], own), group_of, blocks).astype(BF16)
    parts = parts_of(rest) + [jnp.zeros((TAIL - 3, lanes), F32)]
    out_ref[slots:, :] = jnp.concatenate(parts, axis=0).astype(BF16)


def spread(mine, got, mix, shift, blocks):
    slots, lanes = mine.shape
    outs = [((slots + TAIL, lanes), BF16)]
    kernel = functools.partial(spread_kernel, blocks)
    return call(kernel, "spread", outs, [], [mine, got, mix, shift], flops=2 * 10**9)[0]


def update_kernel(blocks, first, side_ref, x_ref, *rest):
    picked_ref, picked_theirs_ref, mine_ref, theirs_ref, out_ref = rest
    half, _, some, local, width = out_ref.shape
    slots = mine_ref.shape[0] - TAIL
    group_of = lane_groups(slots, some, width, blocks)
    sides = ((picked_ref, mine_ref), (picked_theirs_ref, theirs_ref))
    for r, (pick_ref, term_ref) in enumerate(sides):
        j = side_ref[0] ^ r
        terms = term_ref[0:slots, :].astype(F32)
        parts = [jnp.where(group_of == g, terms, 0.0).astype(BF16) for g in range(blocks)]
        update = dot16(pick_ref[...], jnp.concatenate(parts, axis=0))
        tail = term_ref[slots:, :].astype(F32)
        mean_term = (tail[0:1, :] + tail[1:2, :]) + tail[2:3, :]
        result = (side_by_side(x_ref, j, first, some) + mean_term) + update
        for i in range(some):
            piece = result[:, i * width : (i + 1) * width]
            out_ref[:, j, i] = piece.reshape(half, local, width).astype(BF16)


def update(side, x, picked, picked_theirs, terms, got_terms, blocks, first):
    half, two, _, local, width = x.shape
    some = terms.shape[1] // width
    kernel = functools.partial(update_kernel, blocks, first)
    outs = [((half, two, some, local, width), BF16)]
    arrays = [x, picked, picked_theirs, terms, got_terms]
    return call(kernel, "update", outs, [side], arrays, flops=2 * 10**9)[0]


def join_kernel(in_ref, *rest):
    out_ref = rest[-1]
    per_step, _, _, _, width = in_ref.shape
    for q in range(per_step):
        out_ref[:, :, q * width : (q + 1) * width] = in_ref[q, 0]


def join(pieces, chunk, chunks, before):
    half, _, some, local, width = pieces.shape
    per_step = 16 if half % 16 == 0 else half
    steps = half // per_step
    operands = [pieces]
    in_specs = [
        pl.BlockSpec(
            (per_step, 1, some, local, width),
            lambda i: (lax.rem(i, steps), i // steps, 0, 0, 0),
        )
    ]
    if before is not None:
        operands.append(before)
        in_specs.append(pl.BlockSpec(memory_space=pl.ANY))
    return pl.pallas_call(
        join_kernel,
        grid=(2 * steps,),
        in_specs=in_specs,
        out_specs=pl.BlockSpec((some, local, per_step * width), lambda i: (chunk, 0, i)),
        out_shape=jax.ShapeDtypeStruct((some * chunks, local, 2 * half * width), BF16),
        input_output_aliases={} if before is None else {1: 0},
        compiler_params=pltpu.CompilerParams(vmem_limit_bytes=24 * MIB),
        name="join",
    )(*operands)


def shards(ensemble, obs_col, obs_var, obs_value, obs_err, obs_count, coarse_list, coarse_count):
    devices = lax.axis_size("mem") * lax.axis_size("patch")
    half = devices // 2
    me = lax.axis_index(AXES).astype(jnp.int32).reshape(1)
    side = me // half
    local, fields, total = ensemble.shape
    blocks = coarse_list.shape[0]
    by_patch = lambda array: array.reshape(devices, OBS_DEV)
    early = fields // 2
    later = fields - early
    swap = functools.partial(
        lax.all_to_all,
        axis_name=AXES,
        split_axis=0,
        concat_axis=0,
        tiled=True,
        axis_index_groups=[list(range(half)), list(range(half, devices))],
    )
    pairs = [(i, (i + half) % devices) for i in range(devices)]
    cross = lambda array: lax.ppermute(array, AXES, pairs)
    tie = lax.optimization_barrier

    ours = jnp.transpose(ensemble, (1, 0, 2))
    send0, send1 = split(ours, by_patch(obs_var), by_patch(obs_col), devices, early)
    skip = 3 + sum_units(later, local)
    sum_x, x0 = sums(side, swap(send0), coarse_list, later)
    got_x = cross(sum_x)
    picked_theirs, turned_theirs, gram_theirs = picks(1, side, x0, sum_x, got_x, coarse_list)
    got_gram = cross(gram_theirs)
    picked, turned, gram, mean = picks(0, side, x0, sum_x, got_x, coarse_list)
    turns = (sum_x, got_x, turned, turned_theirs, blocks)
    mine0, other0 = project(side, x0, *turns, skip, 3)
    got_other0 = cross(other0)
    got_gram, mine0, send1 = tie((got_gram, mine0, send1))
    x1 = swap(send1)
    mix, shift = weights(
        me,
        obs_count,
        coarse_count,
        coarse_list,
        by_patch(obs_value),
        by_patch(obs_err),
        by_patch(obs_col),
        mean,
        gram,
        got_gram,
        local * devices,
        total,
    )
    terms0 = spread(mine0, got_other0, mix, shift, blocks)
    got_terms0 = cross(terms0)
    terms0, x1 = tie((terms0, x1))
    mine1, other1 = project(side, x1, *turns, 0, 3 + early)
    got_other1 = cross(other1)
    result0 = update(side, x0, picked, picked_theirs, terms0, got_terms0, blocks, skip)
    result0, got_other1 = tie((result0, got_other1))
    terms1 = spread(mine1, got_other1, mix, shift, blocks)
    back0 = swap(result0)
    result1 = update(side, x1, picked, picked_theirs, terms1, cross(terms1), blocks, 0)
    result = join(swap(result1), 1, 2, join(back0, 0, 2, None))
    return jnp.transpose(result, (1, 0, 2))


def solution(mesh):
    return jax.shard_map(
        shards,
        mesh=mesh,
        in_specs=(
            P(AXES, None, None),
            P(),
            P(),
            P(),
            P(),
            P(),
            P(AXES, None),
            P(AXES),
        ),
        out_specs=P(AXES, None, None),
        check_vma=False,
    )
```
